32 devices in a mesh: groups: 2 (over y), tp: 4 (over z), seq: 2 (over x), rep: 2 (over core).
Axes of the slice: x: 2, y: 2, z: 4, core: 2. Of those that a mesh axis runs over, the one named last changes fastest.
Arguments:
- queries: bfloat16 [2048, 8192], P(('groups', 'seq', 'rep'), 'tp'), parts along dimension 0, may hold values from -6 to 6
- keys: bfloat16 [2048, 8, 128], P(('groups', 'seq', 'rep')), parts along dimension 0, may hold values from -6 to 6
- values: bfloat16 [2048, 8, 128], P(('groups', 'seq', 'rep')), parts along dimension 0, may hold values from -18 to 18
- span_order: int32 [8], replicated, may hold values from 0 to 7, each once
- out_weight: bfloat16 [8192, 8192], P('tp', ('seq', 'rep')), may hold values from -0.0625 to 0.0625
- residual: bfloat16 [2048, 8192], P(('groups', 'seq', 'rep'), 'tp'), parts along dimension 0, may hold values from -30 to 30
- norm_gain: bfloat16 [8192], replicated, may hold values from 0.099609375 to 1.8984375
Outputs:
- stream: bfloat16 [2048, 8192], P(('groups', 'seq', 'rep'), 'tp'), parts along dimension 0
- normed: bfloat16 [2048, 8192], P(('groups', 'seq', 'rep')), parts along dimension 0
The draws below stay inside these ranges and needn't reach their ends.
There are 2 independent parts, one for each index of `groups`. The reference program is written for one: setup_inputs(seed, part) draws one part's arguments, and reference() takes and returns one part's arrays. A program takes and returns all parts, laid end to end along the dimension named above; an argument that names none is the same for every part. Nothing has to cross between parts.
Inputs may be any that keep to these rules, and one draw needn't show every extreme that they name: A permutation: row block c of every token array, of 128 rows, holds prompt positions span_order[c] * 128 to span_order[c] * 128 + 127.
All inputs are finite; a program needn't handle non-finite values.
Results may differ from the reference program's by a relative error of at most 0.008.
Values may be sent and summed in bfloat16 or wider, within the bound.
A program may use at most 128 MiB of HBM per device.

```python
import math
import jax
import jax.numpy as jnp
from jax import lax

D = 8192
HQ = 64
KVH = 8
HDIM = 128
TOK_DEV = 256
NCH = 8
TOKENS = 1024
N_TP = 4


def draw_queries(key, part):
    key = jax.random.fold_in(key, 1)
    base = jnp.clip(jax.random.normal(key, (TOKENS, HQ * HDIM), jnp.float32), -6.0, 6.0)
    return base.astype(jnp.bfloat16)


def draw_keys(key, part):
    key = jax.random.fold_in(key, 2)
    base = jnp.clip(jax.random.normal(key, (TOKENS, KVH, HDIM), jnp.float32), -6.0, 6.0)
    return base.astype(jnp.bfloat16)


def draw_residual(key, part):
    key = jax.random.fold_in(key, 3)
    row_key = jax.random.fold_in(key, 4)
    row_scale = jnp.exp(jax.random.uniform(row_key, (TOKENS, 1), jnp.float32, math.log(0.3), math.log(3.0)))
    columns = lax.iota(jnp.int32, D).astype(jnp.float32) / D
    noise = jnp.clip(jax.random.normal(key, (TOKENS, D), jnp.float32), -6.0, 6.0)
    col_scale = 0.15 * jnp.power(10.0, columns)
    return (noise * col_scale[None, :] * row_scale).astype(jnp.bfloat16)


def level_of(key, extent, cuts, smallest, top_value):
    def one(axis_at, blocks):
        draws = jax.random.uniform(jax.random.fold_in(jax.random.fold_in(key, 6), axis_at), (blocks,), jnp.float32, smallest / len(cuts), top_value / len(cuts))
        return jnp.repeat(jnp.exp(draws), extent[axis_at] // blocks).reshape((-1,) + (1,) * (len(extent) - axis_at - 1))

    loudness = one(*cuts[0])
    for cut in cuts[1:]:
        loudness = loudness * one(*cut)
    return loudness


def gaussian(own_key, extent, spread, reach, split=(), held_as=jnp.bfloat16):
    level = level_of(own_key, extent, split, -0.22, 0.18) if split else 1.0
    values = jax.random.normal(own_key, extent, jnp.float32) * spread * level
    return jnp.minimum(jnp.maximum(values, -reach), reach).astype(held_as)


def setup_inputs(seed: int = 0, part: int = 0) -> dict:
    key_list = jax.random.split(jax.random.key(seed), 8)
    part_keys = jax.random.split(jax.random.fold_in(key_list[7], part), 8)
    queries = draw_queries(jax.random.fold_in(jax.random.fold_in(key_list[7], part), 71), part)
    keys = draw_keys(jax.random.fold_in(jax.random.fold_in(key_list[7], part), 71), part)
    values = gaussian(part_keys[2], (TOKENS, KVH, HDIM), 3.0, 18.0, ((0, 4),))
    span_order = jax.random.permutation(key_list[3], NCH).astype(jnp.int32)
    out_weight = gaussian(key_list[4], (HQ * HDIM, D), (HQ * HDIM) ** -0.5, 0.0625, ((0, 4), (1, 4)))
    residual = draw_residual(jax.random.fold_in(jax.random.fold_in(key_list[7], part), 71), part)
    norm_gain = jnp.clip(1.0 + 0.18 * jax.random.normal(key_list[6], (D,), jnp.float32), 0.099609375, 1.8984375).astype(jnp.bfloat16)
    return dict(queries=queries, keys=keys, values=values, span_order=span_order, out_weight=out_weight, residual=residual, norm_gain=norm_gain)


NEG_LARGE = -1e+30
EPS_NORM = 1e-05

def positions(rows, span_order, span_len):
    blocks = rows // span_len
    numbers = lax.iota(jnp.int32, span_order.shape[0])
    chosen = lax.optimization_barrier(jnp.sum(jnp.where(blocks[:, None] == numbers[None, :], span_order[None, :], 0), axis=1)).astype(jnp.int32)
    return (chosen * span_len + rows % span_len).astype(jnp.int32)

def reference(queries, keys, values, span_order, out_weight, residual, norm_gain):
    length = queries.shape[0]
    places = positions(lax.iota(jnp.int32, length), span_order, TOK_DEV // 2)
    allowed = places[None, :] <= places[:, None]
    heads_q = queries.reshape(length, HQ, HDIM).transpose(1, 0, 2)
    heads_k = keys.transpose(1, 0, 2)
    heads_v = values.transpose(1, 0, 2)
    group_size = HQ // KVH
    score_scale = 1.0 / math.sqrt(HDIM)

    def one_head(index):
        query_head = heads_q[index]
        key_head = heads_k[index // group_size]
        value_head = heads_v[index // group_size]
        scores = jnp.dot(query_head, key_head.T, preferred_element_type=jnp.float32) * score_scale
        scores = jnp.where(allowed, scores, NEG_LARGE)
        highest = lax.optimization_barrier(jnp.max(scores, axis=1, keepdims=True))
        expo = jnp.where(allowed, jnp.exp(scores - highest), 0.0)
        totals = lax.optimization_barrier(jnp.sum(expo, axis=1, keepdims=True))
        mixed = jnp.dot(expo.astype(jnp.bfloat16), value_head, preferred_element_type=jnp.float32)
        return mixed / totals
    heads_out = lax.map(one_head, lax.iota(jnp.int32, HQ))
    attention = heads_out.transpose(1, 0, 2).reshape(length, HQ * HDIM).astype(jnp.bfloat16)
    width_tp = HQ * HDIM // N_TP
    pieces_a = attention.reshape(length, N_TP, width_tp).transpose(1, 0, 2)
    pieces_w = out_weight.reshape(N_TP, width_tp, D)

    def add_term(running, pair):
        part_a, part_w = pair
        rounded = jnp.dot(part_a, part_w, preferred_element_type=jnp.float32).astype(jnp.bfloat16)
        return (running + lax.optimization_barrier(rounded).astype(jnp.float32), 0)
    summed, unused = lax.scan(add_term, jnp.zeros((length, D), jnp.float32), (pieces_a, pieces_w))
    stream = (residual.astype(jnp.float32) + summed).astype(jnp.bfloat16)
    stream_wide = stream.astype(jnp.float32)
    inverse = lax.rsqrt(lax.optimization_barrier(jnp.sum(stream_wide * stream_wide, axis=1, keepdims=True)) / D + EPS_NORM)
    scaled = stream_wide * inverse * norm_gain.astype(jnp.float32)[None, :]
    return (stream, scaled.astype(jnp.bfloat16))
```

```python
import math

import jax
import jax.numpy as jnp
from jax import lax
from jax.sharding import PartitionSpec as P

D = 8192
HQ = 64
KVH = 8


NEG_LARGE = -1e30
EPS_NORM = 1e-05


def positions(rows, span_order, span_len):
    blocks = rows // span_len
    numbers = lax.iota(jnp.int32, span_order.shape[0])
    chosen = jnp.sum(jnp.where(blocks[:, None] == numbers[None, :], span_order[None, :], 0), axis=1)
    return chosen * span_len + rows % span_len


def normalize(stream_rows, gain_part, square_total):
    stream_wide = stream_rows.astype(jnp.float32)
    inverse = lax.rsqrt(square_total[:, None] / D + EPS_NORM)
    return (stream_wide * inverse * gain_part.astype(jnp.float32)[None, :]).astype(jnp.bfloat16)


def on_device(queries, keys, values, span_order, out_weight, residual, norm_gain):
    tok_rows = queries.shape[0]
    head_size = keys.shape[2]
    heads_here = queries.shape[1] // head_size
    group_size = HQ // KVH
    per_group = min(group_size, heads_here)
    groups_here = heads_here // per_group
    span_len = tok_rows // 2
    tp_index = lax.axis_index("tp")
    kv_first = tp_index * heads_here // group_size
    key_sel = lax.dynamic_slice_in_dim(keys, kv_first, groups_here, 1).reshape(
        tok_rows, groups_here * head_size
    )
    value_sel = lax.dynamic_slice_in_dim(values, kv_first, groups_here, 1).reshape(
        tok_rows, groups_here * head_size
    )
    seq_index = lax.axis_index(("seq", "rep"))
    query_pos = positions(
        seq_index * tok_rows + lax.iota(jnp.int32, tok_rows), span_order, span_len
    )
    grouped = queries.reshape(tok_rows, groups_here, per_group, head_size)
    score_scale = 1.0 / math.sqrt(head_size)
    key_block = lax.all_gather(key_sel, ("seq", "rep"), axis=0, tiled=True)
    value_block = lax.all_gather(value_sel, ("seq", "rep"), axis=0, tiled=True)
    count = key_block.shape[0]
    key_pos = positions(lax.iota(jnp.int32, count), span_order, span_len)
    best = jnp.full((groups_here, per_group, tok_rows), NEG_LARGE, jnp.float32)
    keys_three = key_block.reshape(count, groups_here, head_size)
    values_three = value_block.reshape(count, groups_here, head_size)
    scores = (
        jnp.einsum("qgrd,kgd->grqk", grouped, keys_three, preferred_element_type=jnp.float32)
        * score_scale
    )
    allowed = key_pos[None, None, None, :] <= query_pos[None, None, :, None]
    scores = jnp.where(allowed, scores, NEG_LARGE)
    new_best = jnp.maximum(best, jnp.max(scores, axis=3))
    expo = jnp.where(allowed, jnp.exp(scores - new_best[..., None]), 0.0)
    new_totals = jnp.sum(expo, axis=3)
    update = jnp.einsum(
        "grqk,kgd->grqd",
        expo.astype(jnp.bfloat16),
        values_three,
        preferred_element_type=jnp.float32,
    )
    attention = (
        (update / new_totals[..., None])
        .transpose(2, 0, 1, 3)
        .reshape(tok_rows, heads_here * head_size)
        .astype(jnp.bfloat16)
    )
    tp_size = lax.axis_size("tp")
    ring = lax.axis_size("seq") * lax.axis_size("rep")
    part_rows = tok_rows // tp_size
    width = residual.shape[1]
    res_rows = lax.all_to_all(
        residual.reshape(tp_size, part_rows, width), "tp", 0, 0, tiled=True
    )
    everyone = lax.all_gather(attention, ("seq", "rep"), axis=0, tiled=True)
    term = jnp.dot(everyone, out_weight, preferred_element_type=jnp.float32).astype(jnp.bfloat16)
    columns = out_weight.shape[1]
    part = lax.psum_scatter(
        term.reshape(ring, tp_size, part_rows, columns), "tp", scatter_dimension=1, tiled=False
    )
    mine = lax.all_to_all(part, ("seq", "rep"), 0, 0, tiled=True)
    summed = mine.transpose(1, 0, 2).reshape(part_rows, D).astype(jnp.float32)
    stream_rows = (
        res_rows.transpose(1, 0, 2).reshape(part_rows, D).astype(jnp.float32) + summed
    ).astype(jnp.bfloat16)
    whole = lax.all_gather(stream_rows, "tp", axis=0, tiled=True)
    wide = whole.astype(jnp.float32)
    normed = normalize(whole, norm_gain, jnp.sum(wide * wide, axis=1))
    stream = lax.dynamic_slice_in_dim(whole, tp_index * width, width, 1)
    return (stream, normed)


def solution(mesh):
    placed = (
        P(("groups", "seq", "rep"), "tp"),
        P(("groups", "seq", "rep"), None, None),
        P(("groups", "seq", "rep"), None, None),
        P(),
        P("tp", ("seq", "rep")),
        P(("groups", "seq", "rep"), "tp"),
        P(),
    )
    return jax.shard_map(
        on_device,
        mesh=mesh,
        in_specs=placed,
        out_specs=(P(("groups", "seq", "rep"), "tp"), P(("groups", "seq", "rep"), None)),
        check_vma=False,
    )
```

```python
import functools
import math

import jax
import jax.numpy as jnp
from jax import lax
from jax.experimental import pallas as pl
from jax.experimental.pallas import tpu as pltpu
from jax.sharding import PartitionSpec as P

D = 8192
HQ = 64
KVH = 8


NEG_LARGE = -1e30
EPS_NORM = 1e-05
MESH = pl.DeviceIdType.MESH


def positions(rows, span_order, span_len):
    blocks = rows // span_len
    numbers = lax.iota(jnp.int32, span_order.shape[0])
    chosen = jnp.sum(jnp.where(blocks[:, None] == numbers[None, :], span_order[None, :], 0), axis=1)
    return chosen * span_len + rows % span_len


def normalize(stream_rows, gain_part, square_total):
    stream_wide = stream_rows.astype(jnp.float32)
    inverse = lax.rsqrt(square_total[:, None] / D + EPS_NORM)
    return (stream_wide * inverse * gain_part.astype(jnp.float32)[None, :]).astype(jnp.bfloat16)


def project_kernel(
    nt, nc, nrep, att, weight, res, gain, stream_o, normed_o,
    term, from_low, from_high, sums_out, sums_in, res_rows, full,
    term_send, low_recv, high_recv, sums_send, sums_recv,
    res_send, res_recv, up_send, down_send, full_recv,
):
    chunks, _, _, rows, width = term.shape
    columns = chunks * width
    t = lax.axis_index("tp")
    c = lax.axis_index("seq") * nrep + lax.axis_index("rep")
    last = nt - 1

    def quad(other):
        return {"seq": other // nrep, "rep": other % nrep}

    barrier = pltpu.get_barrier_semaphore()
    for step in range(1, nt):
        pl.semaphore_signal(
            barrier, inc=1, device_id={"tp": (t + step) % nt}, device_id_type=MESH
        )
    for step in range(1, nc):
        pl.semaphore_signal(
            barrier, inc=1, device_id=quad((c + step) % nc), device_id_type=MESH
        )
    pl.semaphore_wait(barrier, nt + nc - 2)

    def remote(src, dst, send, recv, where):
        return pltpu.make_async_remote_copy(
            src_ref=src, dst_ref=dst, send_sem=send, recv_sem=recv,
            device_id=where, device_id_type=MESH,
        )

    def res_copy(step):
        other = (t + step) % nt
        return remote(
            res.at[pl.ds(pl.multiple_of(other * rows, rows), rows)],
            res_rows.at[t], res_send.at[step], res_recv.at[step], {"tp": other},
        )

    def term_up(k, d):
        return remote(term.at[k, d], from_low.at[k, d], term_send.at[k, d],
                      low_recv.at[k, d], {"tp": (t + 1) % nt})

    def term_down(k, d):
        return remote(term.at[k, d], from_high.at[k, d], term_send.at[k, d],
                      high_recv.at[k, d], {"tp": (t + last) % nt})

    def sums_copy(k, step):
        other = (c + step) % nc
        return remote(sums_out.at[k, other], sums_in.at[k, c], sums_send.at[k, step],
                      sums_recv.at[k, step], quad(other))

    def full_up(k, u):
        return remote(full.at[u, k], full.at[u, k], up_send.at[k, u],
                      full_recv.at[k, u], {"tp": (t + 1) % nt})

    def full_down(k, u):
        return remote(full.at[u, k], full.at[u, k], down_send.at[k, u],
                      full_recv.at[k, u], {"tp": (t + last) % nt})

    def multiply(k):
        part = weight[:, pl.ds(pl.multiple_of(k * width, width), width)]
        for d in range(nt):
            left = att[:, d].reshape(nc * rows, att.shape[3])
            out = jnp.dot(left, part, preferred_element_type=jnp.float32)
            term[k, d] = out.astype(jnp.bfloat16).reshape(nc, rows, width)

        @pl.when(t == 0)
        def _():
            for d in range(last, 0, -1):
                term_up(k, d).start()

        @pl.when(t == last)
        def _():
            for d in range(last):
                term_down(k, d).start()

    def add(x, y):
        return x.astype(jnp.float32) + y.astype(jnp.float32)

    def forward_terms(k):
        for step in range(last):
            d_up, d_down = last - step, step

            @pl.when((t > 0) & (t < d_up))
            def _():
                term_up(k, d_up).wait_recv()
                term[k, d_up] = add(term[k, d_up], from_low[k, d_up]).astype(jnp.bfloat16)
                term_up(k, d_up).start()

            @pl.when((t < last) & (t > d_down))
            def _():
                term_down(k, d_down).wait_recv()
                term[k, d_down] = add(term[k, d_down], from_high[k, d_down]).astype(jnp.bfloat16)
                term_down(k, d_down).start()

    def finish(k):
        @pl.when(t > 0)
        def _():
            term_up(k, t).wait_recv()

        @pl.when(t < last)
        def _():
            term_down(k, t).wait_recv()

        @pl.when(t == 0)
        def _():
            sums_out[k] = add(term[k, t], from_high[k, t]).astype(jnp.bfloat16)

        @pl.when(t == last)
        def _():
            sums_out[k] = add(term[k, t], from_low[k, t]).astype(jnp.bfloat16)

        @pl.when((t > 0) & (t < last))
        def _():
            both = add(term[k, t], from_low[k, t]) + from_high[k, t].astype(jnp.float32)
            sums_out[k] = both.astype(jnp.bfloat16)

        for step in range(1, nc):
            sums_copy(k, step).start()
        sums_in[k, c] = sums_out[k, c]

    def spread(k):
        for step in range(1, nc):
            sums_copy(k, step).wait_recv()
        for block in range(nc):
            held = res_rows[block, :, pl.ds(pl.multiple_of(k * width, width), width)]
            full[t, k, block] = add(held, sums_in[k, block]).astype(jnp.bfloat16)

        @pl.when(t < last)
        def _():
            full_up(k, t).start()

        @pl.when(t > 0)
        def _():
            full_down(k, t).start()

    def forward_full(k):
        for step in range(1, nt):
            @pl.when(t >= step)
            def _():
                u = t - step
                full_up(k, u).wait_recv()

                @pl.when(t < last)
                def _():
                    full_up(k, u).start()

            @pl.when(t + step <= last)
            def _():
                u = t + step
                full_down(k, u).wait_recv()

                @pl.when(t > 0)
                def _():
                    full_down(k, u).start()

    for step in range(1, nt):
        res_copy(step).start()
    res_rows[t] = res[pl.ds(pl.multiple_of(t * rows, rows), rows)]

    def tick(at, carry):
        @pl.when(at < chunks)
        def _():
            multiply(at)
            forward_terms(at)

        @pl.when((at >= 1) & (at <= chunks))
        def _():
            finish(at - 1)

        @pl.when(at == 1)
        def _():
            for step in range(1, nt):
                res_copy(step).wait_recv()

        @pl.when(at >= 2)
        def _():
            forward_full(at - 2)

        @pl.when((at >= 1) & (at <= chunks))
        def _():
            spread(at - 1)

        return carry

    lax.fori_loop(0, chunks + 2, tick, 0)

    def scale_rows(u, carry):
        def squares(k, total):
            piece = full[u, k].astype(jnp.float32)
            return total + jnp.sum(piece * piece, axis=0)

        total = lax.fori_loop(0, chunks, squares, jnp.zeros((rows, width), jnp.float32))
        inverse = lax.rsqrt(jnp.sum(total, axis=1, keepdims=True) / D + EPS_NORM)
        here = pl.ds(pl.multiple_of(u * rows, rows), rows)

        def scale(k, inner):
            for block in range(nc):
                at = pl.ds(pl.multiple_of(block * columns + k * width, width), width)
                wide = full[u, k, block].astype(jnp.float32)
                normed_o[here, at] = (wide * inverse * gain[:, at]).astype(jnp.bfloat16)
            at = pl.ds(pl.multiple_of(k * width, width), width)
            stream_o[here, at] = full[u, k, t]
            return inner

        return lax.fori_loop(0, chunks, scale, carry)

    lax.fori_loop(0, nt, scale_rows, 0)

    for step in range(1, nt):
        res_copy(step).wait_send()

    def drain(k, carry):
        for d in range(nt):
            @pl.when(t != d)
            def _():
                term_up(k, d).wait_send()

            @pl.when((t < last) & (t >= d))
            def _():
                full_up(k, d).wait_send()

            @pl.when((t > 0) & (t <= d))
            def _():
                full_down(k, d).wait_send()

        for step in range(1, nc):
            sums_copy(k, step).wait_send()
        return carry

    lax.fori_loop(0, chunks, drain, 0)


def project(everyone, out_weight, residual, norm_gain, nt, nc, nrep):
    tok_rows, columns = residual.shape
    depth = out_weight.shape[0]
    rows = tok_rows // nt
    width = min(256, columns // 4)
    chunks = columns // width
    bf16 = jnp.bfloat16
    dma = pltpu.SemaphoreType.DMA
    vmem = pl.BlockSpec(memory_space=pltpu.VMEM)
    return pl.pallas_call(
        functools.partial(project_kernel, nt, nc, nrep),
        out_shape=(
            jax.ShapeDtypeStruct((tok_rows, columns), bf16),
            jax.ShapeDtypeStruct((tok_rows, D), bf16),
        ),
        in_specs=[vmem] * 4,
        out_specs=(vmem, vmem),
        scratch_shapes=[
            pltpu.VMEM((chunks, nt, nc, rows, width), bf16),
            pltpu.VMEM((chunks, nt, nc, rows, width), bf16),
            pltpu.VMEM((chunks, nt, nc, rows, width), bf16),
            pltpu.VMEM((chunks, nc, rows, width), bf16),
            pltpu.VMEM((chunks, nc, rows, width), bf16),
            pltpu.VMEM((nt, rows, columns), bf16),
            pltpu.VMEM((nt, chunks, nc, rows, width), bf16),
            dma((chunks, nt)), dma((chunks, nt)), dma((chunks, nt)),
            dma((chunks, nc)), dma((chunks, nc)),
            dma((nt,)), dma((nt,)),
            dma((chunks, nt)), dma((chunks, nt)), dma((chunks, nt)),
        ],
        compiler_params=pltpu.CompilerParams(
            collective_id=0, has_side_effects=True, vmem_limit_bytes=56 * 2**20
        ),
        cost_estimate=pl.CostEstimate(
            flops=2 * nc * tok_rows * depth * columns, bytes_accessed=20 * 2**20, transcendentals=0
        ),
    )(
        everyone.reshape(nc, nt, rows, depth), out_weight, residual,
        norm_gain.astype(jnp.float32).reshape(1, D),
    )


def on_device(queries, keys, values, span_order, out_weight, residual, norm_gain):
    tok_rows = queries.shape[0]
    head_size = keys.shape[2]
    heads_here = queries.shape[1] // head_size
    group_size = HQ // KVH
    per_group = min(group_size, heads_here)
    groups_here = heads_here // per_group
    span_len = tok_rows // 2
    tp_index = lax.axis_index("tp")
    kv_first = tp_index * heads_here // group_size
    key_sel = lax.dynamic_slice_in_dim(keys, kv_first, groups_here, 1).reshape(
        tok_rows, groups_here * head_size
    )
    value_sel = lax.dynamic_slice_in_dim(values, kv_first, groups_here, 1).reshape(
        tok_rows, groups_here * head_size
    )
    seq_index = lax.axis_index(("seq", "rep"))
    query_pos = positions(
        seq_index * tok_rows + lax.iota(jnp.int32, tok_rows), span_order, span_len
    )
    grouped = queries.reshape(tok_rows, groups_here, per_group, head_size)
    score_scale = 1.0 / math.sqrt(head_size)
    key_block = lax.all_gather(key_sel, ("seq", "rep"), axis=0, tiled=True)
    value_block = lax.all_gather(value_sel, ("seq", "rep"), axis=0, tiled=True)
    count = key_block.shape[0]
    key_pos = positions(lax.iota(jnp.int32, count), span_order, span_len)
    best = jnp.full((groups_here, per_group, tok_rows), NEG_LARGE, jnp.float32)
    keys_three = key_block.reshape(count, groups_here, head_size)
    values_three = value_block.reshape(count, groups_here, head_size)
    scores = (
        jnp.einsum("qgrd,kgd->grqk", grouped, keys_three, preferred_element_type=jnp.float32)
        * score_scale
    )
    allowed = key_pos[None, None, None, :] <= query_pos[None, None, :, None]
    scores = jnp.where(allowed, scores, NEG_LARGE)
    new_best = jnp.maximum(best, jnp.max(scores, axis=3))
    expo = jnp.where(allowed, jnp.exp(scores - new_best[..., None]), 0.0)
    new_totals = jnp.sum(expo, axis=3)
    update = jnp.einsum(
        "grqk,kgd->grqd",
        expo.astype(jnp.bfloat16),
        values_three,
        preferred_element_type=jnp.float32,
    )
    attention = (
        (update / new_totals[..., None])
        .transpose(2, 0, 1, 3)
        .reshape(tok_rows, heads_here * head_size)
        .astype(jnp.bfloat16)
    )
    tp_size = lax.axis_size("tp")
    rep_size = lax.axis_size("rep")
    ring = lax.axis_size("seq") * rep_size
    everyone = lax.all_gather(attention, ("seq", "rep"), axis=0, tiled=True)
    return project(everyone, out_weight, residual, norm_gain, tp_size, ring, rep_size)


def solution(mesh):
    placed = (
        P(("groups", "seq", "rep"), "tp"),
        P(("groups", "seq", "rep"), None, None),
        P(("groups", "seq", "rep"), None, None),
        P(),
        P("tp", ("seq", "rep")),
        P(("groups", "seq", "rep"), "tp"),
        P(),
    )
    return jax.shard_map(
        on_device,
        mesh=mesh,
        in_specs=placed,
        out_specs=(P(("groups", "seq", "rep"), "tp"), P(("groups", "seq", "rep"), None)),
        check_vma=False,
    )
```

```python
import functools
import math

import jax
import jax.numpy as jnp
from jax import lax
from jax.experimental import pallas as pl
from jax.experimental.pallas import tpu as pltpu
from jax.sharding import PartitionSpec as P

D = 8192
HQ = 64
KVH = 8


NEG_LARGE = -1e30
EPS_NORM = 1e-05
LAG_TERMS, LAG_SUMS, LAG_SPREAD, LAG_FULL = 1, 2, 2, 3
WIDTH = 512
MESH = pl.DeviceIdType.MESH


def positions(rows, span_order, span_len):
    blocks = rows // span_len
    numbers = lax.iota(jnp.int32, span_order.shape[0])
    chosen = jnp.sum(jnp.where(blocks[:, None] == numbers[None, :], span_order[None, :], 0), axis=1)
    return chosen * span_len + rows % span_len


def normalize(stream_rows, gain_part, square_total):
    stream_wide = stream_rows.astype(jnp.float32)
    inverse = lax.rsqrt(square_total[:, None] / D + EPS_NORM)
    return (stream_wide * inverse * gain_part.astype(jnp.float32)[None, :]).astype(jnp.bfloat16)


def project_kernel(
    nt, nc, nrep, att, weight, res, gain, stream_o, normed_o,
    term, from_low, from_high, sums_out, sums_in, res_rows, full,
    term_send, low_recv, high_recv, sums_send, sums_recv,
    res_send, res_recv, up_send, down_send, full_recv,
):
    chunks, _, _, rows, width = term.shape
    columns = chunks * width
    t = lax.axis_index("tp")
    c = lax.axis_index("seq") * nrep + lax.axis_index("rep")
    last = nt - 1

    def quad(other):
        return {"seq": other // nrep, "rep": other % nrep}

    barrier = pltpu.get_barrier_semaphore()
    for step in range(1, nt):
        pl.semaphore_signal(
            barrier, inc=1, device_id={"tp": (t + step) % nt}, device_id_type=MESH
        )
    for step in range(1, nc):
        pl.semaphore_signal(
            barrier, inc=1, device_id=quad((c + step) % nc), device_id_type=MESH
        )
    pl.semaphore_wait(barrier, nt + nc - 2)

    def remote(src, dst, send, recv, where):
        return pltpu.make_async_remote_copy(
            src_ref=src, dst_ref=dst, send_sem=send, recv_sem=recv,
            device_id=where, device_id_type=MESH,
        )

    def res_copy(step):
        other = (t + step) % nt
        return remote(
            res.at[pl.ds(pl.multiple_of(other * rows, rows), rows)],
            res_rows.at[t], res_send.at[step], res_recv.at[step], {"tp": other},
        )

    def term_up(k, d):
        return remote(term.at[k, d], from_low.at[k, d], term_send.at[k, d],
                      low_recv.at[k, d], {"tp": (t + 1) % nt})

    def term_down(k, d):
        return remote(term.at[k, d], from_high.at[k, d], term_send.at[k, d],
                      high_recv.at[k, d], {"tp": (t + last) % nt})

    def sums_copy(k, step):
        other = (c + step) % nc
        return remote(sums_out.at[k, other], sums_in.at[k, c], sums_send.at[k, step],
                      sums_recv.at[k, step], quad(other))

    def full_up(k, u):
        return remote(full.at[u, k], full.at[u, k], up_send.at[k, u],
                      full_recv.at[k, u], {"tp": (t + 1) % nt})

    def full_down(k, u):
        return remote(full.at[u, k], full.at[u, k], down_send.at[k, u],
                      full_recv.at[k, u], {"tp": (t + last) % nt})

    def multiply(k):
        part = weight[:, pl.ds(pl.multiple_of(k * width, width), width)]
        for d in range(nt):
            left = att[:, d].reshape(nc * rows, att.shape[3])
            out = jnp.dot(left, part, preferred_element_type=jnp.float32)
            term[k, d] = out.astype(jnp.bfloat16).reshape(nc, rows, width)

        @pl.when(t == 0)
        def _():
            for d in range(last, 0, -1):
                term_up(k, d).start()

        @pl.when(t == last)
        def _():
            for d in range(last):
                term_down(k, d).start()

    def add(x, y):
        return x.astype(jnp.float32) + y.astype(jnp.float32)

    def forward_terms(k):
        for step in range(last):
            d_up, d_down = last - step, step

            @pl.when((t > 0) & (t < d_up))
            def _():
                term_up(k, d_up).wait_recv()
                term[k, d_up] = add(term[k, d_up], from_low[k, d_up]).astype(jnp.bfloat16)
                term_up(k, d_up).start()

            @pl.when((t < last) & (t > d_down))
            def _():
                term_down(k, d_down).wait_recv()
                term[k, d_down] = add(term[k, d_down], from_high[k, d_down]).astype(jnp.bfloat16)
                term_down(k, d_down).start()

    def finish(k):
        @pl.when(t > 0)
        def _():
            term_up(k, t).wait_recv()

        @pl.when(t < last)
        def _():
            term_down(k, t).wait_recv()

        @pl.when(t == 0)
        def _():
            sums_out[k] = add(term[k, t], from_high[k, t]).astype(jnp.bfloat16)

        @pl.when(t == last)
        def _():
            sums_out[k] = add(term[k, t], from_low[k, t]).astype(jnp.bfloat16)

        @pl.when((t > 0) & (t < last))
        def _():
            both = add(term[k, t], from_low[k, t]) + from_high[k, t].astype(jnp.float32)
            sums_out[k] = both.astype(jnp.bfloat16)

        for step in range(1, nc):
            sums_copy(k, step).start()
        sums_in[k, c] = sums_out[k, c]

    def spread(k):
        for step in range(1, nc):
            sums_copy(k, step).wait_recv()
        for block in range(nc):
            held = res_rows[block, :, pl.ds(pl.multiple_of(k * width, width), width)]
            full[t, k, block] = add(held, sums_in[k, block]).astype(jnp.bfloat16)

        @pl.when(t < last)
        def _():
            full_up(k, t).start()

        @pl.when(t > 0)
        def _():
            full_down(k, t).start()

    def forward_full(k):
        for step in range(1, nt):
            @pl.when(t >= step)
            def _():
                u = t - step
                full_up(k, u).wait_recv()

                @pl.when(t < last)
                def _():
                    full_up(k, u).start()

            @pl.when(t + step <= last)
            def _():
                u = t + step
                full_down(k, u).wait_recv()

                @pl.when(t > 0)
                def _():
                    full_down(k, u).start()

    for step in range(1, nt):
        res_copy(step).start()
    res_rows[t] = res[pl.ds(pl.multiple_of(t * rows, rows), rows)]

    def get_res(k):
        @pl.when(k == 0)
        def _():
            for step in range(1, nt):
                res_copy(step).wait_recv()

    stages = (
        (0, multiply), (LAG_TERMS, forward_terms), (LAG_SUMS, finish),
        (LAG_FULL, forward_full), (LAG_SPREAD, get_res), (LAG_SPREAD, spread),
    )

    def tick(at, carry):
        for lag, stage in stages:
            @pl.when((at >= lag) & (at < chunks + lag))
            def _():
                stage(at - lag)

        return carry

    lax.fori_loop(0, chunks + LAG_FULL, tick, 0)

    def scale_rows(u, carry):
        def squares(k, total):
            piece = full[u, k].astype(jnp.float32)
            return total + jnp.sum(piece * piece, axis=0)

        total = lax.fori_loop(0, chunks, squares, jnp.zeros((rows, width), jnp.float32))
        inverse = lax.rsqrt(jnp.sum(total, axis=1, keepdims=True) / D + EPS_NORM)
        here = pl.ds(pl.multiple_of(u * rows, rows), rows)

        def scale(k, inner):
            for block in range(nc):
                at = pl.ds(pl.multiple_of(block * columns + k * width, width), width)
                wide = full[u, k, block].astype(jnp.float32)
                normed_o[here, at] = (wide * inverse * gain[:, at]).astype(jnp.bfloat16)
            at = pl.ds(pl.multiple_of(k * width, width), width)
            stream_o[here, at] = full[u, k, t]
            return inner

        return lax.fori_loop(0, chunks, scale, carry)

    lax.fori_loop(0, nt, scale_rows, 0)

    for step in range(1, nt):
        res_copy(step).wait_send()

    def drain(k, carry):
        for d in range(nt):
            @pl.when(t != d)
            def _():
                term_up(k, d).wait_send()

            @pl.when((t < last) & (t >= d))
            def _():
                full_up(k, d).wait_send()

            @pl.when((t > 0) & (t <= d))
            def _():
                full_down(k, d).wait_send()

        for step in range(1, nc):
            sums_copy(k, step).wait_send()
        return carry

    lax.fori_loop(0, chunks, drain, 0)


def project(everyone, out_weight, residual, norm_gain, nt, nc, nrep):
    tok_rows, columns = residual.shape
    depth = out_weight.shape[0]
    rows = tok_rows // nt
    width = min(WIDTH, columns // 4)
    chunks = columns // width
    bf16 = jnp.bfloat16
    dma = pltpu.SemaphoreType.DMA
    vmem = pl.BlockSpec(memory_space=pltpu.VMEM)
    return pl.pallas_call(
        functools.partial(project_kernel, nt, nc, nrep),
        out_shape=(
            jax.ShapeDtypeStruct((tok_rows, columns), bf16),
            jax.ShapeDtypeStruct((tok_rows, D), bf16),
        ),
        in_specs=[vmem] * 4,
        out_specs=(vmem, vmem),
        scratch_shapes=[
            pltpu.VMEM((chunks, nt, nc, rows, width), bf16),
            pltpu.VMEM((chunks, nt, nc, rows, width), bf16),
            pltpu.VMEM((chunks, nt, nc, rows, width), bf16),
            pltpu.VMEM((chunks, nc, rows, width), bf16),
            pltpu.VMEM((chunks, nc, rows, width), bf16),
            pltpu.VMEM((nt, rows, columns), bf16),
            pltpu.VMEM((nt, chunks, nc, rows, width), bf16),
            dma((chunks, nt)), dma((chunks, nt)), dma((chunks, nt)),
            dma((chunks, nc)), dma((chunks, nc)),
            dma((nt,)), dma((nt,)),
            dma((chunks, nt)), dma((chunks, nt)), dma((chunks, nt)),
        ],
        compiler_params=pltpu.CompilerParams(
            collective_id=0, has_side_effects=True, vmem_limit_bytes=56 * 2**20
        ),
        cost_estimate=pl.CostEstimate(
            flops=2 * nc * tok_rows * depth * columns, bytes_accessed=20 * 2**20, transcendentals=0
        ),
    )(
        everyone.reshape(nc, nt, rows, depth), out_weight, residual,
        norm_gain.astype(jnp.float32).reshape(1, D),
    )


def on_device(queries, keys, values, span_order, out_weight, residual, norm_gain):
    tok_rows = queries.shape[0]
    head_size = keys.shape[2]
    heads_here = queries.shape[1] // head_size
    group_size = HQ // KVH
    per_group = min(group_size, heads_here)
    groups_here = heads_here // per_group
    span_len = tok_rows // 2
    tp_index = lax.axis_index("tp")
    kv_first = tp_index * heads_here // group_size
    key_sel = lax.dynamic_slice_in_dim(keys, kv_first, groups_here, 1).reshape(
        tok_rows, groups_here * head_size
    )
    value_sel = lax.dynamic_slice_in_dim(values, kv_first, groups_here, 1).reshape(
        tok_rows, groups_here * head_size
    )
    seq_index = lax.axis_index(("seq", "rep"))
    query_pos = positions(
        seq_index * tok_rows + lax.iota(jnp.int32, tok_rows), span_order, span_len
    )
    grouped = queries.reshape(tok_rows, groups_here, per_group, head_size)
    score_scale = 1.0 / math.sqrt(head_size)
    both = lax.all_gather(
        jnp.concatenate([key_sel, value_sel], axis=1), ("seq", "rep"), axis=0, tiled=True
    )
    key_block, value_block = jnp.split(both, 2, axis=1)
    count = key_block.shape[0]
    key_pos = positions(lax.iota(jnp.int32, count), span_order, span_len)
    best = jnp.full((groups_here, per_group, tok_rows), NEG_LARGE, jnp.float32)
    keys_three = key_block.reshape(count, groups_here, head_size)
    values_three = value_block.reshape(count, groups_here, head_size)
    scores = (
        jnp.einsum("qgrd,kgd->grqk", grouped, keys_three, preferred_element_type=jnp.float32)
        * score_scale
    )
    allowed = key_pos[None, None, None, :] <= query_pos[None, None, :, None]
    scores = jnp.where(allowed, scores, NEG_LARGE)
    new_best = jnp.maximum(best, jnp.max(scores, axis=3))
    expo = jnp.where(allowed, jnp.exp(scores - new_best[..., None]), 0.0)
    new_totals = jnp.sum(expo, axis=3)
    update = jnp.einsum(
        "grqk,kgd->grqd",
        expo.astype(jnp.bfloat16),
        values_three,
        preferred_element_type=jnp.float32,
    )
    attention = (
        (update / new_totals[..., None])
        .transpose(2, 0, 1, 3)
        .reshape(tok_rows, heads_here * head_size)
        .astype(jnp.bfloat16)
    )
    tp_size = lax.axis_size("tp")
    rep_size = lax.axis_size("rep")
    ring = lax.axis_size("seq") * rep_size
    everyone = lax.all_gather(attention, ("seq", "rep"), axis=0, tiled=True)
    return project(everyone, out_weight, residual, norm_gain, tp_size, ring, rep_size)


def solution(mesh):
    placed = (
        P(("groups", "seq", "rep"), "tp"),
        P(("groups", "seq", "rep"), None, None),
        P(("groups", "seq", "rep"), None, None),
        P(),
        P("tp", ("seq", "rep")),
        P(("groups", "seq", "rep"), "tp"),
        P(),
    )
    return jax.shard_map(
        on_device,
        mesh=mesh,
        in_specs=placed,
        out_specs=(P(("groups", "seq", "rep"), "tp"), P(("groups", "seq", "rep"), None)),
        check_vma=False,
    )
```

```python
import functools
import math

import jax
import jax.numpy as jnp
from jax import lax
from jax.experimental import pallas as pl
from jax.experimental.pallas import tpu as pltpu
from jax.sharding import PartitionSpec as P

D = 8192
HQ = 64
KVH = 8


NEG_LARGE = -1e30
EPS_NORM = 1e-05
LAG_TERMS, LAG_SUMS, LAG_SPREAD, LAG_FULL = 1, 2, 2, 3
WIDTH = 512
MESH = pl.DeviceIdType.MESH


def positions(rows, span_order, span_len):
    blocks = rows // span_len
    numbers = lax.iota(jnp.int32, span_order.shape[0])
    chosen = jnp.sum(jnp.where(blocks[:, None] == numbers[None, :], span_order[None, :], 0), axis=1)
    return chosen * span_len + rows % span_len


def normalize(stream_rows, gain_part, square_total):
    stream_wide = stream_rows.astype(jnp.float32)
    inverse = lax.rsqrt(square_total[:, None] / D + EPS_NORM)
    return (stream_wide * inverse * gain_part.astype(jnp.float32)[None, :]).astype(jnp.bfloat16)


def project_kernel(
    nt, nc, nrep, own, weight, res, gain, stream_o, normed_o,
    att, term, from_low, from_high, sums_out, sums_in, res_rows, full,
    term_send, low_recv, high_recv, sums_send, sums_recv,
    res_send, res_recv, up_send, down_send, full_recv,
    seq_send, core_send, att_recv,
):
    chunks, _, _, rows, width = term.shape
    columns = chunks * width
    t = lax.axis_index("tp")
    c = lax.axis_index("seq") * nrep + lax.axis_index("rep")
    last = nt - 1

    def quad(other):
        return {"seq": other // nrep, "rep": other % nrep}

    barrier = pltpu.get_barrier_semaphore()
    for step in range(1, nt):
        pl.semaphore_signal(
            barrier, inc=1, device_id={"tp": (t + step) % nt}, device_id_type=MESH
        )
    for step in range(1, nc):
        pl.semaphore_signal(
            barrier, inc=1, device_id=quad((c + step) % nc), device_id_type=MESH
        )
    pl.semaphore_wait(barrier, nt + nc - 2)

    def remote(src, dst, send, recv, where):
        return pltpu.make_async_remote_copy(
            src_ref=src, dst_ref=dst, send_sem=send, recv_sem=recv,
            device_id=where, device_id_type=MESH,
        )

    def res_copy(step):
        other = (t + step) % nt
        return remote(
            res.at[pl.ds(pl.multiple_of(other * rows, rows), rows)],
            res_rows.at[t], res_send.at[step], res_recv.at[step], {"tp": other},
        )

    def term_up(k, d):
        return remote(term.at[k, d], from_low.at[k, d], term_send.at[k, d],
                      low_recv.at[k, d], {"tp": (t + 1) % nt})

    def term_down(k, d):
        return remote(term.at[k, d], from_high.at[k, d], term_send.at[k, d],
                      high_recv.at[k, d], {"tp": (t + last) % nt})

    def sums_copy(k, step):
        other = (c + step) % nc
        return remote(sums_out.at[k, other], sums_in.at[k, c], sums_send.at[k, step],
                      sums_recv.at[k, step], quad(other))

    def full_up(k, u):
        return remote(full.at[u, k], full.at[u, k], up_send.at[k, u],
                      full_recv.at[k, u], {"tp": (t + 1) % nt})

    def full_down(k, u):
        return remote(full.at[u, k], full.at[u, k], down_send.at[k, u],
                      full_recv.at[k, u], {"tp": (t + last) % nt})

    seq, core = lax.axis_index("seq"), lax.axis_index("rep")
    nseq = nc // nrep

    def across(d, step):
        return remote(att.at[c, d], att.at[c, d], seq_send.at[d, step],
                      att_recv.at[d, c], {"seq": (seq + step) % nseq})

    def share(d, place, step):
        block = place * nrep + core
        return remote(att.at[block, d], att.at[block, d], core_send.at[d, place, step],
                      att_recv.at[d, block], {"rep": (core + step) % nrep})

    def arrived(d, block):
        remote(att.at[block, d], att.at[block, d], seq_send.at[d, 0],
               att_recv.at[d, block], {"seq": (seq + 1) % nseq}).wait_recv()

    def send_own(d, carry):
        att[c, d] = own[d]
        for step in range(1, nseq):
            across(d, step).start()
        for step in range(1, nrep):
            share(d, seq, step).start()
        return carry

    def pass_on(d, carry):
        for step in range(1, nseq):
            place = (seq + nseq - step) % nseq
            arrived(d, place * nrep + core)
            for other in range(1, nrep):
                share(d, place, other).start()
        return carry

    def collect(d, carry):
        for other in range(1, nrep):
            for place in range(nseq):
                arrived(d, place * nrep + (core + other) % nrep)
        return carry

    def att_sent(d, carry):
        for step in range(1, nseq):
            across(d, step).wait_send()
        for place in range(nseq):
            for other in range(1, nrep):
                share(d, place, other).wait_send()
        return carry

    def multiply(k):
        part = weight[:, pl.ds(pl.multiple_of(k * width, width), width)]
        for d in range(nt):
            left = att[:, d].reshape(nc * rows, att.shape[3])
            out = jnp.dot(left, part, preferred_element_type=jnp.float32)
            term[k, d] = out.astype(jnp.bfloat16).reshape(nc, rows, width)

        @pl.when(t == 0)
        def _():
            for d in range(last, 0, -1):
                term_up(k, d).start()

        @pl.when(t == last)
        def _():
            for d in range(last):
                term_down(k, d).start()

    def add(x, y):
        return x.astype(jnp.float32) + y.astype(jnp.float32)

    def forward_terms(k):
        for step in range(last):
            d_up, d_down = last - step, step

            @pl.when((t > 0) & (t < d_up))
            def _():
                term_up(k, d_up).wait_recv()
                term[k, d_up] = add(term[k, d_up], from_low[k, d_up]).astype(jnp.bfloat16)
                term_up(k, d_up).start()

            @pl.when((t < last) & (t > d_down))
            def _():
                term_down(k, d_down).wait_recv()
                term[k, d_down] = add(term[k, d_down], from_high[k, d_down]).astype(jnp.bfloat16)
                term_down(k, d_down).start()

    def finish(k):
        @pl.when(t > 0)
        def _():
            term_up(k, t).wait_recv()

        @pl.when(t < last)
        def _():
            term_down(k, t).wait_recv()

        @pl.when(t == 0)
        def _():
            sums_out[k] = add(term[k, t], from_high[k, t]).astype(jnp.bfloat16)

        @pl.when(t == last)
        def _():
            sums_out[k] = add(term[k, t], from_low[k, t]).astype(jnp.bfloat16)

        @pl.when((t > 0) & (t < last))
        def _():
            both = add(term[k, t], from_low[k, t]) + from_high[k, t].astype(jnp.float32)
            sums_out[k] = both.astype(jnp.bfloat16)

        for step in range(1, nc):
            sums_copy(k, step).start()
        sums_in[k, c] = sums_out[k, c]

    def spread(k):
        for step in range(1, nc):
            sums_copy(k, step).wait_recv()
        for block in range(nc):
            held = res_rows[block, :, pl.ds(pl.multiple_of(k * width, width), width)]
            full[t, k, block] = add(held, sums_in[k, block]).astype(jnp.bfloat16)

        @pl.when(t < last)
        def _():
            full_up(k, t).start()

        @pl.when(t > 0)
        def _():
            full_down(k, t).start()

    def forward_full(k):
        for step in range(1, nt):
            @pl.when(t >= step)
            def _():
                u = t - step
                full_up(k, u).wait_recv()

                @pl.when(t < last)
                def _():
                    full_up(k, u).start()

            @pl.when(t + step <= last)
            def _():
                u = t + step
                full_down(k, u).wait_recv()

                @pl.when(t > 0)
                def _():
                    full_down(k, u).start()

    lax.fori_loop(0, nt, send_own, 0)
    for step in range(1, nt):
        res_copy(step).start()
    res_rows[t] = res[pl.ds(pl.multiple_of(t * rows, rows), rows)]

    def get_res(k):
        @pl.when(k == 0)
        def _():
            for step in range(1, nt):
                res_copy(step).wait_recv()

    stages = (
        (0, multiply), (LAG_TERMS, forward_terms), (LAG_SUMS, finish),
        (LAG_FULL, forward_full), (LAG_SPREAD, get_res), (LAG_SPREAD, spread),
    )

    lax.fori_loop(0, nt, pass_on, 0)
    lax.fori_loop(0, nt, collect, 0)

    def tick(at, carry):
        for lag, stage in stages:
            @pl.when((at >= lag) & (at < chunks + lag))
            def _():
                stage(at - lag)

        return carry

    lax.fori_loop(0, chunks + LAG_FULL, tick, 0)

    def scale_rows(u, carry):
        def squares(k, total):
            piece = full[u, k].astype(jnp.float32)
            return total + jnp.sum(piece * piece, axis=0)

        total = lax.fori_loop(0, chunks, squares, jnp.zeros((rows, width), jnp.float32))
        inverse = lax.rsqrt(jnp.sum(total, axis=1, keepdims=True) / D + EPS_NORM)
        here = pl.ds(pl.multiple_of(u * rows, rows), rows)

        def scale(k, inner):
            for block in range(nc):
                at = pl.ds(pl.multiple_of(block * columns + k * width, width), width)
                wide = full[u, k, block].astype(jnp.float32)
                normed_o[here, at] = (wide * inverse * gain[:, at]).astype(jnp.bfloat16)
            at = pl.ds(pl.multiple_of(k * width, width), width)
            stream_o[here, at] = full[u, k, t]
            return inner

        return lax.fori_loop(0, chunks, scale, carry)

    lax.fori_loop(0, nt, scale_rows, 0)

    for step in range(1, nt):
        res_copy(step).wait_send()

    def drain(k, carry):
        for d in range(nt):
            @pl.when(t != d)
            def _():
                term_up(k, d).wait_send()

            @pl.when((t < last) & (t >= d))
            def _():
                full_up(k, d).wait_send()

            @pl.when((t > 0) & (t <= d))
            def _():
                full_down(k, d).wait_send()

        for step in range(1, nc):
            sums_copy(k, step).wait_send()
        return carry

    lax.fori_loop(0, chunks, drain, 0)
    lax.fori_loop(0, nt, att_sent, 0)


def project(attention, out_weight, residual, norm_gain, nt, nc, nrep):
    tok_rows, columns = residual.shape
    depth = out_weight.shape[0]
    rows = tok_rows // nt
    width = min(WIDTH, columns // 4)
    chunks = columns // width
    bf16 = jnp.bfloat16
    dma = pltpu.SemaphoreType.DMA
    vmem = pl.BlockSpec(memory_space=pltpu.VMEM)
    return pl.pallas_call(
        functools.partial(project_kernel, nt, nc, nrep),
        out_shape=(
            jax.ShapeDtypeStruct((tok_rows, columns), bf16),
            jax.ShapeDtypeStruct((tok_rows, D), bf16),
        ),
        in_specs=[vmem] * 4,
        out_specs=(vmem, vmem),
        scratch_shapes=[
            pltpu.VMEM((nc, nt, rows, depth), bf16),
            pltpu.VMEM((chunks, nt, nc, rows, width), bf16),
            pltpu.VMEM((chunks, nt, nc, rows, width), bf16),
            pltpu.VMEM((chunks, nt, nc, rows, width), bf16),
            pltpu.VMEM((chunks, nc, rows, width), bf16),
            pltpu.VMEM((chunks, nc, rows, width), bf16),
            pltpu.VMEM((nt, rows, columns), bf16),
            pltpu.VMEM((nt, chunks, nc, rows, width), bf16),
            dma((chunks, nt)), dma((chunks, nt)), dma((chunks, nt)),
            dma((chunks, nc)), dma((chunks, nc)),
            dma((nt,)), dma((nt,)),
            dma((chunks, nt)), dma((chunks, nt)), dma((chunks, nt)),
            dma((nt, nc // nrep)), dma((nt, nc // nrep, nrep)), dma((nt, nc)),
        ],
        compiler_params=pltpu.CompilerParams(
            collective_id=0, has_side_effects=True, vmem_limit_bytes=56 * 2**20
        ),
        cost_estimate=pl.CostEstimate(
            flops=2 * nc * tok_rows * depth * columns, bytes_accessed=20 * 2**20, transcendentals=0
        ),
    )(
        attention.reshape(nt, rows, depth), out_weight, residual,
        norm_gain.astype(jnp.float32).reshape(1, D),
    )


def on_device(queries, keys, values, span_order, out_weight, residual, norm_gain):
    tok_rows = queries.shape[0]
    head_size = keys.shape[2]
    heads_here = queries.shape[1] // head_size
    group_size = HQ // KVH
    per_group = min(group_size, heads_here)
    groups_here = heads_here // per_group
    span_len = tok_rows // 2
    tp_index = lax.axis_index("tp")
    kv_first = tp_index * heads_here // group_size
    key_sel = lax.dynamic_slice_in_dim(keys, kv_first, groups_here, 1).reshape(
        tok_rows, groups_here * head_size
    )
    value_sel = lax.dynamic_slice_in_dim(values, kv_first, groups_here, 1).reshape(
        tok_rows, groups_here * head_size
    )
    seq_index = lax.axis_index(("seq", "rep"))
    query_pos = positions(
        seq_index * tok_rows + lax.iota(jnp.int32, tok_rows), span_order, span_len
    )
    grouped = queries.reshape(tok_rows, groups_here, per_group, head_size)
    score_scale = 1.0 / math.sqrt(head_size)
    both = lax.all_gather(
        jnp.concatenate([key_sel, value_sel], axis=1), ("seq", "rep"), axis=0, tiled=True
    )
    key_block, value_block = jnp.split(both, 2, axis=1)
    count = key_block.shape[0]
    key_pos = positions(lax.iota(jnp.int32, count), span_order, span_len)
    best = jnp.full((groups_here, per_group, tok_rows), NEG_LARGE, jnp.float32)
    keys_three = key_block.reshape(count, groups_here, head_size)
    values_three = value_block.reshape(count, groups_here, head_size)
    scores = (
        jnp.einsum("qgrd,kgd->grqk", grouped, keys_three, preferred_element_type=jnp.float32)
        * score_scale
    )
    allowed = key_pos[None, None, None, :] <= query_pos[None, None, :, None]
    scores = jnp.where(allowed, scores, NEG_LARGE)
    new_best = jnp.maximum(best, jnp.max(scores, axis=3))
    expo = jnp.where(allowed, jnp.exp(scores - new_best[..., None]), 0.0)
    new_totals = jnp.sum(expo, axis=3)
    update = jnp.einsum(
        "grqk,kgd->grqd",
        expo.astype(jnp.bfloat16),
        values_three,
        preferred_element_type=jnp.float32,
    )
    attention = (
        (update / new_totals[..., None])
        .transpose(2, 0, 1, 3)
        .reshape(tok_rows, heads_here * head_size)
        .astype(jnp.bfloat16)
    )
    tp_size = lax.axis_size("tp")
    rep_size = lax.axis_size("rep")
    ring = lax.axis_size("seq") * rep_size
    return project(attention, out_weight, residual, norm_gain, tp_size, ring, rep_size)


def solution(mesh):
    placed = (
        P(("groups", "seq", "rep"), "tp"),
        P(("groups", "seq", "rep"), None, None),
        P(("groups", "seq", "rep"), None, None),
        P(),
        P("tp", ("seq", "rep")),
        P(("groups", "seq", "rep"), "tp"),
        P(),
    )
    return jax.shard_map(
        on_device,
        mesh=mesh,
        in_specs=placed,
        out_specs=(P(("groups", "seq", "rep"), "tp"), P(("groups", "seq", "rep"), None)),
        check_vma=False,
    )
```
